32 devices in a mesh: bank: 8 (over z, y), tp: 4 (over x, core).
Axes of the slice: x: 2, y: 2, z: 4, core: 2. Of those that a mesh axis runs over, the one named last changes fastest.
Arguments:
- hidden: bfloat16 [16, 512, 14336], P('bank', None, 'tp'), may hold values from -6 to 6
- out_grad: bfloat16 [16, 512, 4096], P('bank', None, 'tp'), may hold values from -6 to 6
- proj_in: bfloat16 [64, 14336], P(None, 'tp'), may hold values from -0.046875 to 0.046875
- proj_out: bfloat16 [64, 4096], P(None, 'tp'), may hold values from -0.09375 to 0.09375
- lengths: int32 [16], P('bank'), may hold values from 1 to 512, 6144 in all
- pair_perm: int32 [16], replicated, may hold values from 0 to 15, each once
- bank_slab: bfloat16 [8192, 4096], P('bank', 'tp'), may hold values from -6 to 6
Outputs:
- scores: float32 [8, 8192], P('tp', 'bank')
The draws below stay inside these ranges and needn't reach their ends.
Inputs may be any that keep to these rules, and one draw needn't show every extreme that they name: pair_perm holds every variant index exactly once. `lengths`: some prompt fills all 512 slots.
All inputs are finite; a program needn't handle non-finite values. No bound on the sum of `lengths` on one device may be relied on, other than what follows from the above.
Results may differ from the reference program's by a relative error of at most 0.0029.
Values sent between devices are 32-bit elements; how exact they have to be, the bound alone decides.
No kernel may reach another device: no remote copies, remote signals or barrier semaphores. Data moves between devices by JAX's collectives and lax.ppermute only.
A program may use at most 64 MiB of HBM per device.

```python
import math
import jax
import jax.numpy as jnp
import numpy as np
from jax import lax

D = 4096
FF = 14336
RANK = 64
SEQ = 512
EXAMPLES = 16
BANK_ROWS = 8192


def level_of(own_key, extent, split, least, largest):
    level = 1.0
    for position, parts in split:
        heights = jax.random.uniform(jax.random.fold_in(jax.random.fold_in(own_key, 6), position), (parts,), jnp.float32, least / len(split), largest / len(split))
        level = level * jnp.repeat(jnp.exp(heights), extent[position] // parts).reshape((-1,) + (1,) * (len(extent) - 1 - position))
    return level


def length_profile(amount, total, limit, skew):
    loads = [(1 << 20) // math.isqrt(rank ** skew) + 1 for rank in range(2, amount + 1)]
    surplus, counts = total - limit - (amount - 1), [1] * (amount - 1)
    while surplus > 0:
        candidates = [i for i in range(amount - 1) if counts[i] < limit]
        whole, remaining = sum([loads[i] for i in candidates]), surplus
        for i in candidates:
            more = min(limit - counts[i], max(1, remaining * loads[i] // whole), surplus)
            counts[i] = counts[i] + more
            surplus = surplus - more
    return np.array([limit] + counts)


def uneven(stream_key, count, total, reach, skew):
    if count == 2:
        one = jax.random.randint(stream_key, (), max(1, total - reach), min(reach, total - 1) + 1)
        return jnp.stack([one, total - one])
    sizes = jnp.asarray(length_profile(count, total, reach, skew), jnp.int32)
    couples = (count - 1) // 2
    donor, sink = sizes[1:1 + 2 * couples:2], sizes[2:2 + 2 * couples:2]
    room = jnp.minimum(donor - 1, reach - sink)
    moved = jax.random.randint(jax.random.fold_in(stream_key, 1), (couples,), 0, 1 << 20) % (room + 1)
    sizes = sizes.at[1:1 + 2 * couples:2].set(donor - moved).at[2:2 + 2 * couples:2].set(sink + moved)
    return sizes[jax.random.permutation(jax.random.fold_in(stream_key, 2), count)]


def noise(key, dims, scale, reach, pieces=(), held_as=jnp.bfloat16):
    level = level_of(key, dims, pieces, -0.22, 0.18) if pieces else 1.0
    values = jax.random.normal(key, dims, jnp.float32) * scale * level
    return jnp.minimum(jnp.maximum(values, -reach), reach).astype(held_as)


def setup_inputs(seed: int = 0) -> dict:
    key_of = jax.random.split(jax.random.key(seed), 8)
    return {
        "hidden": noise(key_of[0], (EXAMPLES, SEQ, FF), 1.0, 6.0, ((0, 8), (2, 4))),
        "out_grad": noise(key_of[1], (EXAMPLES, SEQ, D), 1.0, 6.0, ((0, 8), (2, 4))),
        "proj_in": noise(key_of[2], (RANK, FF), FF ** -0.5, 0.046875, ((1, 4),)),
        "proj_out": noise(key_of[3], (RANK, D), D ** -0.5, 0.09375, ((1, 4),)),
        "lengths": uneven(key_of[4], EXAMPLES, EXAMPLES * (SEQ // 2 + SEQ // 4), SEQ, 0).astype(jnp.int32),
        "pair_perm": jax.random.permutation(key_of[5], EXAMPLES).astype(jnp.int32),
        "bank_slab": noise(key_of[6], (BANK_ROWS, RANK * RANK), 1.0, 6.0, ((0, 8), (1, 4))),
    }


epsilon = 1e-06

def reference(hidden, out_grad, proj_in, proj_out, lengths, pair_perm, bank_slab):
    positions = jnp.arange(SEQ, dtype=jnp.int32)

    def one_example(packed):
        hid_rows, grad_rows, length_one = packed
        in_factor = jnp.dot(hid_rows, proj_in.T, preferred_element_type=jnp.float32)
        out_factor = jnp.dot(grad_rows, proj_out.T, preferred_element_type=jnp.float32)
        live_mask = (positions < length_one).astype(jnp.float32)
        masked = in_factor * live_mask[:, None]
        outer = jnp.dot(masked.T, out_factor, precision=lax.Precision.HIGHEST)
        return outer.reshape(RANK * RANK)
    grads = lax.map(one_example, (hidden, out_grad, lengths))
    benign = pair_perm[0::2]
    harmful = pair_perm[1::2]
    queries = grads[harmful] - grads[benign]
    query_sq = lax.optimization_barrier(jnp.sum(queries * queries, axis=1))
    slab_wide = bank_slab.astype(jnp.float32)
    bank_sq = lax.optimization_barrier(jnp.sum(slab_wide * slab_wide, axis=1))
    query_low = queries.astype(jnp.bfloat16)
    dots = lax.dot_general(query_low, bank_slab, (((1,), (1,)), ((), ())), preferred_element_type=jnp.float32)
    return dots * RANK * lax.rsqrt(query_sq + epsilon)[:, None] * lax.rsqrt(bank_sq + epsilon)[None, :]
```

```python
import jax
import jax.numpy as jnp
from jax import lax
from jax.sharding import PartitionSpec as P

epsilon = 1e-06


def flip(step):
    return [(i, i ^ step) for i in range(4)]


def per_device(hidden, out_grad, proj_in, proj_out, lengths, pair_perm, bank_slab):
    ex_dev, seq_len, _ = hidden.shape
    factor_rank = proj_in.shape[0]
    tp_count = lax.axis_size("tp")
    bank_count = lax.axis_size("bank")
    k = lax.axis_index("tp")
    core = lax.rem(k, 2)
    share_rows = factor_rank // tp_count

    def pick(arr, which):
        return lax.dynamic_index_in_dim(arr, which, 0, keepdims=False)

    def factor(proj, rows):
        return jnp.einsum("rf,tf->rt", proj, rows, preferred_element_type=jnp.float32)

    out_send = factor(proj_out, pick(out_grad, 1 - core))
    out_keep = factor(proj_out, pick(out_grad, core))
    out_chip = out_keep + lax.ppermute(out_send, "tp", flip(1))
    out_full = out_chip + lax.ppermute(out_chip, "tp", flip(2))
    in_send = factor(proj_in, pick(hidden, 1 - core))
    in_keep = factor(proj_in, pick(hidden, core))
    in_chip = in_keep + lax.ppermute(in_send, "tp", flip(1))
    positions = jnp.arange(seq_len, dtype=jnp.int32)
    live_mask = (positions < pick(lengths, core)).astype(jnp.float32)
    grads = jnp.einsum(
        "it,jt->ij", in_chip * live_mask[None, :], out_full, precision=lax.Precision.HIGHEST
    )
    cols = share_rows * factor_rank
    outgoing = jnp.broadcast_to(
        grads.reshape(1, tp_count, cols), (bank_count, tp_count, cols)
    ).reshape(bank_count * tp_count, cols)
    partials = lax.all_to_all(outgoing, ("bank", "tp"), 0, 0, tiled=True)
    source = jnp.arange(bank_count * tp_count, dtype=jnp.int32)
    example_ids = (source // tp_count) * ex_dev + source % 2
    pair_count = pair_perm.shape[0] // 2
    pairs_mine = pair_count // tp_count
    order = jnp.arange(pair_count, dtype=jnp.int32)
    pair_ids = ((order // pairs_mine) ^ k) * pairs_mine + order % pairs_mine
    benign = pair_perm[0::2][pair_ids]
    harmful = pair_perm[1::2][pair_ids]
    pair_signs = (example_ids[None, :] == harmful[:, None]).astype(jnp.float32) - (
        example_ids[None, :] == benign[:, None]
    ).astype(jnp.float32)
    queries = jnp.dot(pair_signs, partials, precision=lax.Precision.HIGHEST)
    query_part = jnp.sum(queries * queries, axis=1)
    slab_wide = bank_slab.astype(jnp.float32)
    bank_part = jnp.sum(slab_wide * slab_wide, axis=1)
    dots = lax.dot_general(
        queries.astype(jnp.bfloat16),
        bank_slab,
        (((1,), (1,)), ((), ())),
        preferred_element_type=jnp.float32,
    )
    rows = bank_slab.shape[0]
    message = jnp.concatenate(
        [
            dots.reshape(tp_count, pairs_mine, rows),
            jnp.broadcast_to(bank_part[None, None, :], (tp_count, 1, rows)),
            jnp.pad(
                query_part.reshape(tp_count, 1, pairs_mine), ((0, 0), (0, 0), (0, rows - pairs_mine))
            ),
        ],
        axis=1,
    )
    total = message[0]
    for step in range(1, 4):
        total = total + lax.ppermute(message[step], "tp", flip(step))
    query_sq = total[pairs_mine + 1, :pairs_mine]
    bank_sq = total[pairs_mine]
    return (
        total[:pairs_mine]
        * factor_rank
        * lax.rsqrt(query_sq + epsilon)[:, None]
        * lax.rsqrt(bank_sq + epsilon)[None, :]
    )


def solution(mesh):
    return jax.shard_map(
        per_device,
        mesh=mesh,
        in_specs=(
            P("bank", None, "tp"),
            P("bank", None, "tp"),
            P(None, "tp"),
            P(None, "tp"),
            P("bank"),
            P(),
            P("bank", "tp"),
        ),
        out_specs=P("tp", "bank"),
        check_vma=False,
    )
```

```python
import functools

import jax
import jax.numpy as jnp
from jax import lax
from jax.experimental import pallas as pl
from jax.experimental.pallas import tpu as pltpu
from jax.sharding import PartitionSpec as P

epsilon = 1e-06
VMEM = pl.BlockSpec(memory_space=pltpu.VMEM)
ANY = pl.BlockSpec(memory_space=pl.ANY)
CHUNKS = 2
SMEM = pl.BlockSpec(memory_space=pltpu.SMEM)


def flip(step):
    return [(i, i ^ step) for i in range(4)]


def put_factor(rows, proj, out_ref, start):
    part = lax.dot_general(
        rows, proj, (((1,), (1,)), ((), ())), preferred_element_type=jnp.float32
    )
    out_ref[:, start : start + rows.shape[0]] = part.T


def in_hbm(arr):
    return pltpu.with_memory_space_constraint(arr, pltpu.HBM)


def out_send_kernel(proj_ref, rows_ref, send_ref, proj_held, rows_held, rows_buf, sems):
    core = lax.rem(lax.axis_index("tp"), 2)
    copies = [
        pltpu.make_async_copy(proj_ref, proj_held, sems.at[0]),
        pltpu.make_async_copy(rows_ref.at[1 - core], rows_buf, sems.at[1]),
        pltpu.make_async_copy(rows_ref.at[core], rows_held, sems.at[2]),
    ]
    for copy in copies:
        copy.start()
    for copy in copies:
        copy.wait()
    put_factor(rows_buf[...], proj_held[...], send_ref, 0)


def out_send(proj, rows):
    rank, depth = proj.shape
    _, tokens, _ = rows.shape
    return pl.pallas_call(
        out_send_kernel,
        out_shape=[
            jax.ShapeDtypeStruct((rank, tokens), jnp.float32),
            jax.ShapeDtypeStruct(proj.shape, proj.dtype),
            jax.ShapeDtypeStruct((tokens, depth), rows.dtype),
        ],
        in_specs=[ANY, ANY],
        out_specs=[VMEM, VMEM, VMEM],
        scratch_shapes=[pltpu.VMEM((tokens, depth), rows.dtype), pltpu.SemaphoreType.DMA((3,))],
        compiler_params=pltpu.CompilerParams(vmem_limit_bytes=8 << 20),
        cost_estimate=pl.CostEstimate(
            flops=4 * rank * depth * tokens, bytes_accessed=4 * depth * tokens, transcendentals=0
        ),
    )(in_hbm(proj), in_hbm(rows))


def out_keep_kernel(proj_ref, rows_ref, out_ref):
    put_factor(rows_ref[...], proj_ref[...], out_ref, 0)


def out_keep(proj, rows):
    rank, depth = proj.shape
    tokens, _ = rows.shape
    return pl.pallas_call(
        out_keep_kernel,
        out_shape=jax.ShapeDtypeStruct((rank, tokens), jnp.float32),
        in_specs=[VMEM, VMEM],
        out_specs=VMEM,
        compiler_params=pltpu.CompilerParams(vmem_limit_bytes=8 << 20),
        cost_estimate=pl.CostEstimate(
            flops=4 * rank * depth * tokens, bytes_accessed=2 * depth * tokens, transcendentals=0
        ),
    )(proj, rows)


def add_kernel(left_ref, right_ref, out_ref):
    out_ref[...] = left_ref[...] + right_ref[...]


def add(left, right):
    return pl.pallas_call(
        add_kernel,
        out_shape=jax.ShapeDtypeStruct(left.shape, left.dtype),
        in_specs=[VMEM, VMEM],
        out_specs=VMEM,
        compiler_params=pltpu.CompilerParams(vmem_limit_bytes=4 << 20),
        cost_estimate=pl.CostEstimate(flops=4 * 10**9, bytes_accessed=16 << 20, transcendentals=0),
    )(left, right)


def in_kernel(proj_ref, rows_ref, after_ref, send_ref, keep_ref):
    core = lax.rem(lax.axis_index("tp"), 2)
    tokens = rows_ref.shape[1]
    for swap, out_ref in ((1, send_ref), (0, keep_ref)):
        prompt = lax.rem(core + swap, 2)
        for start in range(0, tokens, 256):
            put_factor(rows_ref[prompt, start : start + 256, :], proj_ref[...], out_ref, start)


def in_factors(proj, rows, after):
    rank, depth = proj.shape
    tokens = rows.shape[1]
    return pl.pallas_call(
        in_kernel,
        out_shape=[jax.ShapeDtypeStruct((rank, tokens), jnp.float32)] * 2,
        in_specs=[VMEM, VMEM, ANY],
        out_specs=[VMEM, VMEM],
        compiler_params=pltpu.CompilerParams(vmem_limit_bytes=8 << 20),
        cost_estimate=pl.CostEstimate(
            flops=8 * rank * depth * tokens, bytes_accessed=4 * depth * tokens, transcendentals=0
        ),
    )(proj, rows, after)


def outer_kernel(lengths_ref, in_keep_ref, in_got_ref, out_chip_ref, out_got_ref, send_ref, grads_ref):
    rank, tokens = in_keep_ref.shape
    which = lax.rem(lax.axis_index("tp"), 2)
    positions = lax.broadcasted_iota(jnp.int32, (rank, tokens), 1)
    in_chip = in_keep_ref[...] + in_got_ref[...]
    masked = jnp.where(positions < lengths_ref[which], in_chip, 0.0)
    out_full = out_chip_ref[...] + out_got_ref[...]
    grads_ref[...] = lax.dot_general(
        masked,
        out_full,
        (((1,), (1,)), ((), ())),
        precision=lax.Precision.HIGHEST,
        preferred_element_type=jnp.float32,
    )
    half = rank // 2
    even = grads_ref[pl.ds(0, half, stride=2), :]
    odd = grads_ref[pl.ds(1, half, stride=2), :]
    packed = jnp.concatenate([even, odd], axis=1)
    for target in range(send_ref.shape[0]):
        share = target % 4
        send_ref[target] = packed[share * 8 : share * 8 + 8, :]


def outer(lengths, in_keep, in_got, out_chip, out_got, targets):
    rank, tokens = in_keep.shape
    return pl.pallas_call(
        outer_kernel,
        out_shape=jax.ShapeDtypeStruct((targets, rank // 8, 2 * rank), jnp.float32),
        in_specs=[SMEM, VMEM, VMEM, VMEM, VMEM],
        out_specs=VMEM,
        scratch_shapes=[pltpu.VMEM((rank, rank), jnp.float32)],
        compiler_params=pltpu.CompilerParams(vmem_limit_bytes=8 << 20),
        cost_estimate=pl.CostEstimate(
            flops=12 * rank * rank * tokens, bytes_accessed=4 * rank * tokens, transcendentals=0
        ),
    )(lengths, in_keep, in_got, out_chip, out_got)


def norm_kernel(slab_ref, out_ref, held_ref, sems):
    rows, cols = slab_ref.shape
    step = rows // CHUNKS
    copies = []
    for at in range(CHUNKS):
        span = pl.ds(at * step, step)
        copy = pltpu.make_async_copy(slab_ref.at[span, :], held_ref.at[span, :], sems.at[at])
        copy.start()
        copies.append(copy)
    for chunk, copy in enumerate(copies):
        copy.wait()
        for start in range(chunk * step, (chunk + 1) * step, 128):
            total = jnp.zeros((128, 128), jnp.float32)
            for at in range(0, cols, 128):
                wide = held_ref[start : start + 128, at : at + 128].astype(jnp.float32)
                total = total + wide * wide
            out_ref[:, start : start + 128] = jnp.sum(total.T, axis=0, keepdims=True)


def norms(slab):
    rows, cols = slab.shape
    return pl.pallas_call(
        norm_kernel,
        out_shape=[
            jax.ShapeDtypeStruct((1, rows), jnp.float32),
            jax.ShapeDtypeStruct((rows, cols), slab.dtype),
        ],
        in_specs=[ANY],
        out_specs=[VMEM, VMEM],
        scratch_shapes=[pltpu.SemaphoreType.DMA((CHUNKS,))],
        compiler_params=pltpu.CompilerParams(vmem_limit_bytes=8 << 20),
        cost_estimate=pl.CostEstimate(
            flops=2 * rows * cols, bytes_accessed=2 * rows * cols, transcendentals=0
        ),
    )(in_hbm(slab))


def dots_kernel(pairs_mine, perm_ref, partials_ref, slab_ref, norm_ref, *refs):
    *message_refs, query_ref = refs
    k = lax.axis_index("tp")
    pair_count = query_ref.shape[0]

    def whole(example):
        row = (example // 2) * 4 + lax.rem(example, 2)
        return partials_ref[row] + partials_ref[row + 2]

    for at in range(pair_count):
        pair = (k ^ (at // pairs_mine)) * pairs_mine + at % pairs_mine
        query_ref[at] = whole(perm_ref[2 * pair + 1]) - whole(perm_ref[2 * pair])
    depth = query_ref.shape[1]
    blocks = [query_ref[:, r, :] for r in range(depth)]
    queries = jnp.concatenate(blocks, axis=1)
    query_sq = jnp.sum(queries * queries, axis=1, keepdims=True)
    dots = lax.dot_general(
        queries.astype(jnp.bfloat16),
        slab_ref[...],
        (((1,), (1,)), ((), ())),
        preferred_element_type=jnp.float32,
    )
    rows = slab_ref.shape[0]
    for step, message_ref in enumerate(message_refs):
        mine = slice(step * pairs_mine, (step + 1) * pairs_mine)
        message_ref[0:pairs_mine, 0:rows] = dots[mine]
        message_ref[pairs_mine : pairs_mine + 1, 0:rows] = norm_ref[...]
        message_ref[0:pairs_mine, rows : rows + 128] = jnp.broadcast_to(query_sq[mine], (pairs_mine, 128))
        message_ref[pairs_mine : pairs_mine + 1, rows : rows + 128] = jnp.zeros((1, 128), jnp.float32)


def dots(pair_perm, partials, slab, bank_part, tp_count):
    pair_count = pair_perm.shape[0] // 2
    pairs_mine = pair_count // tp_count
    rows, cols = slab.shape
    message = jax.ShapeDtypeStruct((pairs_mine + 1, rows + 128), jnp.float32)
    return pl.pallas_call(
        functools.partial(dots_kernel, pairs_mine),
        out_shape=[message] * tp_count,
        in_specs=[SMEM, VMEM, VMEM, VMEM],
        out_specs=[VMEM] * tp_count,
        scratch_shapes=[pltpu.VMEM((pair_count, 8, 128), jnp.float32)],
        compiler_params=pltpu.CompilerParams(vmem_limit_bytes=8 << 20),
        cost_estimate=pl.CostEstimate(
            flops=2 * pair_count * rows * cols, bytes_accessed=2 * rows * cols, transcendentals=0
        ),
    )(pair_perm, partials, slab, bank_part)


def scores_kernel(scale, own_ref, *refs):
    *got_refs, out_ref = refs
    total = own_ref[...]
    for got_ref in got_refs:
        total = total + got_ref[...]
    pairs, rows = out_ref.shape
    bank_scale = lax.rsqrt(total[pairs : pairs + 1, 0:rows] + epsilon)
    query_scale = lax.rsqrt(total[0:pairs, rows : rows + 1] + epsilon)
    out_ref[...] = total[0:pairs, 0:rows] * scale * query_scale * bank_scale


def scores(messages, scale):
    pairs = messages[0].shape[0] - 1
    rows = messages[0].shape[1] - 128
    return pl.pallas_call(
        functools.partial(scores_kernel, scale),
        out_shape=jax.ShapeDtypeStruct((pairs, rows), jnp.float32),
        in_specs=[VMEM] * len(messages),
        out_specs=VMEM,
        compiler_params=pltpu.CompilerParams(vmem_limit_bytes=8 << 20),
    )(*messages)


def per_device(hidden, out_grad, proj_in, proj_out, lengths, pair_perm, bank_slab):
    rank = proj_in.shape[0]
    tp_count = lax.axis_size("tp")
    bank_count = lax.axis_size("bank")
    out_away, proj_held, rows_held = out_send(proj_out, out_grad)
    out_got = lax.ppermute(out_away, "tp", flip(1))
    out_chip = add(out_keep(proj_held, rows_held), out_got)
    out_other = lax.ppermute(out_chip, "tp", flip(2))
    in_send, in_keep = in_factors(proj_in, hidden, out_chip)
    in_got = lax.ppermute(in_send, "tp", flip(1))
    outgoing = outer(lengths, in_keep, in_got, out_chip, out_other, bank_count * tp_count)
    partials = lax.all_to_all(outgoing, ("bank", "tp"), 0, 0, tiled=True)
    bank_part, held = norms(bank_slab)
    messages = dots(pair_perm, partials, held, bank_part, tp_count)
    got = [messages[0]] + [lax.ppermute(messages[step], "tp", flip(step)) for step in range(1, 4)]
    return scores(got, float(rank))


def solution(mesh):
    return jax.shard_map(
        per_device,
        mesh=mesh,
        in_specs=(
            P("bank", None, "tp"),
            P("bank", None, "tp"),
            P(None, "tp"),
            P(None, "tp"),
            P("bank"),
            P(),
            P("bank", "tp"),
        ),
        out_specs=P("tp", "bank"),
        check_vma=False,
    )
```

```python
import functools

import jax
import jax.numpy as jnp
from jax import lax
from jax.experimental import pallas as pl
from jax.experimental.pallas import tpu as pltpu
from jax.sharding import PartitionSpec as P

epsilon = 1e-06
VMEM = pl.BlockSpec(memory_space=pltpu.VMEM)
ANY = pl.BlockSpec(memory_space=pl.ANY)


def flip(step):
    return [(i, i ^ step) for i in range(4)]


def put_factor(rows, proj, out_ref, start):
    part = lax.dot_general(
        rows, proj, (((1,), (1,)), ((), ())), preferred_element_type=jnp.float32
    )
    out_ref[:, start : start + rows.shape[0]] = part.T


def in_hbm(arr):
    return pltpu.with_memory_space_constraint(arr, pltpu.HBM)


def out_send_kernel(proj_ref, rows_ref, send_ref, proj_held, rows_held, rows_buf, sems):
    core = lax.rem(lax.axis_index("tp"), 2)
    copies = [
        pltpu.make_async_copy(rows_ref.at[1 - core], rows_buf, sems.at[0]),
        pltpu.make_async_copy(proj_ref, proj_held, sems.at[1]),
        pltpu.make_async_copy(rows_ref.at[core], rows_held, sems.at[2]),
    ]
    for copy in copies:
        copy.start()
    copies[0].wait()
    copies[1].wait()
    put_factor(rows_buf[...], proj_held[...], send_ref, 0)
    copies[2].wait()


def out_send(proj, rows):
    rank, depth = proj.shape
    _, tokens, _ = rows.shape
    return pl.pallas_call(
        out_send_kernel,
        out_shape=[
            jax.ShapeDtypeStruct((rank, tokens), jnp.float32),
            jax.ShapeDtypeStruct(proj.shape, proj.dtype),
            jax.ShapeDtypeStruct((tokens, depth), rows.dtype),
        ],
        in_specs=[ANY, ANY],
        out_specs=[VMEM, VMEM, VMEM],
        scratch_shapes=[pltpu.VMEM((tokens, depth), rows.dtype), pltpu.SemaphoreType.DMA((3,))],
        compiler_params=pltpu.CompilerParams(vmem_limit_bytes=8 << 20),
        cost_estimate=pl.CostEstimate(
            flops=4 * rank * depth * tokens, bytes_accessed=4 * depth * tokens, transcendentals=0
        ),
    )(in_hbm(proj), in_hbm(rows))


def out_keep_kernel(proj_ref, rows_ref, out_ref):
    put_factor(rows_ref[...], proj_ref[...], out_ref, 0)


def out_keep(proj, rows):
    rank, depth = proj.shape
    tokens, _ = rows.shape
    return pl.pallas_call(
        out_keep_kernel,
        out_shape=jax.ShapeDtypeStruct((rank, tokens), jnp.float32),
        in_specs=[VMEM, VMEM],
        out_specs=VMEM,
        compiler_params=pltpu.CompilerParams(vmem_limit_bytes=8 << 20),
        cost_estimate=pl.CostEstimate(
            flops=4 * rank * depth * tokens, bytes_accessed=2 * depth * tokens, transcendentals=0
        ),
    )(proj, rows)


def add_kernel(left_ref, right_ref, *refs):
    out_ref = refs[-1]
    out_ref[...] = left_ref[...] + right_ref[...]


def add(left, right, *after):
    return pl.pallas_call(
        add_kernel,
        out_shape=jax.ShapeDtypeStruct(left.shape, left.dtype),
        in_specs=[VMEM, VMEM] + [ANY] * len(after),
        out_specs=VMEM,
        compiler_params=pltpu.CompilerParams(vmem_limit_bytes=4 << 20),
        cost_estimate=pl.CostEstimate(flops=4 * 10**9, bytes_accessed=16 << 20, transcendentals=0),
    )(left, right, *after)


def in_kernel(proj_ref, rows_ref, after_ref, send_ref, keep_ref):
    core = lax.rem(lax.axis_index("tp"), 2)
    tokens = rows_ref.shape[1]
    for swap, out_ref in ((1, send_ref), (0, keep_ref)):
        prompt = lax.rem(core + swap, 2)
        for start in range(0, tokens, 256):
            put_factor(rows_ref[prompt, start : start + 256, :], proj_ref[...], out_ref, start)


def in_factors(proj, rows, after):
    rank, depth = proj.shape
    tokens = rows.shape[1]
    return pl.pallas_call(
        in_kernel,
        out_shape=[jax.ShapeDtypeStruct((rank, tokens), jnp.float32)] * 2,
        in_specs=[VMEM, VMEM, ANY],
        out_specs=[VMEM, VMEM],
        compiler_params=pltpu.CompilerParams(vmem_limit_bytes=8 << 20),
        cost_estimate=pl.CostEstimate(
            flops=8 * rank * depth * tokens, bytes_accessed=4 * depth * tokens, transcendentals=0
        ),
    )(proj, rows, after)


def outer_kernel(live_ref, in_keep_ref, in_got_ref, out_chip_ref, out_got_ref, after_ref, send_ref, grads_ref):
    rank = in_keep_ref.shape[0]
    masked = jnp.where(live_ref[...] > 0.0, in_keep_ref[...] + in_got_ref[...], 0.0)
    out_full = out_chip_ref[...] + out_got_ref[...]
    grads_ref[...] = lax.dot_general(
        masked,
        out_full,
        (((1,), (1,)), ((), ())),
        precision=lax.Precision.HIGHEST,
        preferred_element_type=jnp.float32,
    )
    half = rank // 2
    even = grads_ref[pl.ds(0, half, stride=2), :]
    odd = grads_ref[pl.ds(1, half, stride=2), :]
    packed = jnp.concatenate([even, odd], axis=1)
    for target in range(send_ref.shape[0]):
        share = target % 4
        send_ref[target] = packed[share * 8 : share * 8 + 8, :]


def outer(live, in_keep, in_got, out_chip, out_got, after, targets):
    rank, tokens = in_keep.shape
    return pl.pallas_call(
        outer_kernel,
        out_shape=jax.ShapeDtypeStruct((targets, rank // 8, 2 * rank), jnp.float32),
        in_specs=[VMEM, VMEM, VMEM, VMEM, VMEM, ANY],
        out_specs=VMEM,
        scratch_shapes=[pltpu.VMEM((rank, rank), jnp.float32)],
        compiler_params=pltpu.CompilerParams(vmem_limit_bytes=8 << 20),
        cost_estimate=pl.CostEstimate(
            flops=12 * rank * rank * tokens, bytes_accessed=4 * rank * tokens, transcendentals=0
        ),
    )(live, in_keep, in_got, out_chip, out_got, after)


def norm_kernel(slab_ref, after_ref, out_ref):
    rows, cols = slab_ref.shape
    for start in range(0, rows, 128):
        total = jnp.zeros((128, 128), jnp.float32)
        for at in range(0, cols, 128):
            wide = slab_ref[start : start + 128, at : at + 128].astype(jnp.float32)
            total = total + wide * wide
        out_ref[:, start : start + 128] = jnp.sum(total.T, axis=0, keepdims=True)


def norms(slab, after):
    rows, cols = slab.shape
    return pl.pallas_call(
        norm_kernel,
        out_shape=jax.ShapeDtypeStruct((1, rows), jnp.float32),
        in_specs=[VMEM, ANY],
        out_specs=VMEM,
        compiler_params=pltpu.CompilerParams(vmem_limit_bytes=8 << 20),
        cost_estimate=pl.CostEstimate(
            flops=2 * rows * cols, bytes_accessed=2 * rows * cols, transcendentals=0
        ),
    )(slab, after)


def dots_kernel(signs_ref, partials_ref, slab_ref, norm_ref, *message_refs):
    pair_count = signs_ref.shape[0]
    pairs_mine = pair_count // len(message_refs)
    rows = slab_ref.shape[0]
    blocks = [partials_ref[:, r, :] for r in range(partials_ref.shape[1])]
    partials = jnp.concatenate(blocks, axis=1)
    queries = lax.dot_general(
        signs_ref[...],
        partials,
        (((1,), (0,)), ((), ())),
        precision=lax.Precision.HIGHEST,
        preferred_element_type=jnp.float32,
    )
    query_sq = jnp.sum(queries * queries, axis=1, keepdims=True)
    dots = lax.dot_general(
        queries.astype(jnp.bfloat16),
        slab_ref[...],
        (((1,), (1,)), ((), ())),
        preferred_element_type=jnp.float32,
    )
    for step, message_ref in enumerate(message_refs):
        mine = slice(step * pairs_mine, (step + 1) * pairs_mine)
        message_ref[0:pairs_mine, 0:rows] = dots[mine]
        message_ref[pairs_mine : pairs_mine + 1, 0:rows] = norm_ref[...]
        message_ref[0:pairs_mine, rows : rows + 128] = jnp.broadcast_to(query_sq[mine], (pairs_mine, 128))
        message_ref[pairs_mine : pairs_mine + 1, rows : rows + 128] = jnp.zeros((1, 128), jnp.float32)


def dots(signs, partials, slab, bank_part, tp_count):
    pair_count = signs.shape[0]
    rows, cols = slab.shape
    message = jax.ShapeDtypeStruct((pair_count // tp_count + 1, rows + 128), jnp.float32)
    return pl.pallas_call(
        dots_kernel,
        out_shape=[message] * tp_count,
        in_specs=[VMEM, VMEM, VMEM, VMEM],
        out_specs=[VMEM] * tp_count,
        compiler_params=pltpu.CompilerParams(vmem_limit_bytes=8 << 20),
        cost_estimate=pl.CostEstimate(
            flops=2 * pair_count * rows * cols, bytes_accessed=2 * rows * cols, transcendentals=0
        ),
    )(signs, partials, slab, bank_part)


def pair_signs(pair_perm, sources, tp_count):
    slots = jnp.arange(pair_perm.shape[0], dtype=jnp.int32)
    pair_count = pair_perm.shape[0] // 2
    pairs_mine = pair_count // tp_count
    order = jnp.arange(pair_count, dtype=jnp.int32)
    pair = ((order // pairs_mine) ^ lax.axis_index("tp")) * pairs_mine + order % pairs_mine
    weights = (slots[None, :] == 2 * pair[:, None] + 1).astype(jnp.float32) - (
        slots[None, :] == 2 * pair[:, None]
    ).astype(jnp.float32)
    source = jnp.arange(sources, dtype=jnp.int32)
    example = (source // tp_count) * 2 + source % 2
    hits = (pair_perm[None, :, None] == example[None, None, :]).astype(jnp.float32)
    return jnp.sum(weights[:, :, None] * hits, axis=1)


def scores_kernel(scale, own_ref, *refs):
    *got_refs, out_ref = refs
    total = own_ref[...]
    for got_ref in got_refs:
        total = total + got_ref[...]
    pairs, rows = out_ref.shape
    bank_scale = lax.rsqrt(total[pairs : pairs + 1, 0:rows] + epsilon)
    query_scale = lax.rsqrt(total[0:pairs, rows : rows + 1] + epsilon)
    out_ref[...] = total[0:pairs, 0:rows] * scale * query_scale * bank_scale


def scores(messages, scale):
    pairs = messages[0].shape[0] - 1
    rows = messages[0].shape[1] - 128
    return pl.pallas_call(
        functools.partial(scores_kernel, scale),
        out_shape=jax.ShapeDtypeStruct((pairs, rows), jnp.float32),
        in_specs=[VMEM] * len(messages),
        out_specs=VMEM,
        compiler_params=pltpu.CompilerParams(vmem_limit_bytes=8 << 20),
    )(*messages)


def live_row(lengths, tokens):
    prompts = jnp.arange(lengths.shape[0], dtype=jnp.int32)
    positions = jnp.arange(tokens, dtype=jnp.int32)
    mine = prompts == lax.rem(lax.axis_index("tp"), 2)
    live = mine[:, None] & (positions[None, :] < lengths[:, None])
    return jnp.sum(live.astype(jnp.float32), axis=0, keepdims=True)


def per_device(hidden, out_grad, proj_in, proj_out, lengths, pair_perm, bank_slab):
    rank = proj_in.shape[0]
    tp_count = lax.axis_size("tp")
    bank_count = lax.axis_size("bank")
    live = live_row(lengths, hidden.shape[1])
    signs = pair_signs(pair_perm, bank_count * tp_count, tp_count)
    out_away, proj_held, rows_held = out_send(proj_out, out_grad)
    out_got = lax.ppermute(out_away, "tp", flip(1))
    out_chip = add(out_keep(proj_held, rows_held), out_got, live, signs)
    out_other = lax.ppermute(out_chip, "tp", flip(2))
    in_away, in_keep = in_factors(proj_in, hidden, out_chip)
    in_got = lax.ppermute(in_away, "tp", flip(1))
    bank_part = norms(bank_slab, in_away)
    outgoing = outer(live, in_keep, in_got, out_chip, out_other, bank_part, bank_count * tp_count)
    partials = lax.all_to_all(outgoing, ("bank", "tp"), 0, 0, tiled=True)
    messages = dots(signs, partials, bank_slab, bank_part, tp_count)
    got = [messages[0]] + [lax.ppermute(messages[step], "tp", flip(step)) for step in range(1, 4)]
    return scores(got, float(rank))


def solution(mesh):
    return jax.shard_map(
        per_device,
        mesh=mesh,
        in_specs=(
            P("bank", None, "tp"),
            P("bank", None, "tp"),
            P(None, "tp"),
            P(None, "tp"),
            P("bank"),
            P(),
            P("bank", "tp"),
        ),
        out_specs=P("tp", "bank"),
        check_vma=False,
    )
```

```python
import functools

import jax
import jax.numpy as jnp
from jax import lax
from jax.experimental import pallas as pl
from jax.experimental.pallas import tpu as pltpu
from jax.sharding import PartitionSpec as P

epsilon = 1e-06
VMEM = pl.BlockSpec(memory_space=pltpu.VMEM)
ANY = pl.BlockSpec(memory_space=pl.ANY)


def flip(step):
    return [(i, i ^ step) for i in range(4)]


def put_factor(rows, proj, out_ref, start):
    part = lax.dot_general(
        rows, proj, (((1,), (1,)), ((), ())), preferred_element_type=jnp.float32
    )
    out_ref[:, start : start + rows.shape[0]] = part.T


def in_hbm(arr):
    return pltpu.with_memory_space_constraint(arr, pltpu.HBM)


def out_send_kernel(
    pairs_mine, proj_ref, rows_ref, lengths_ref, perm_ref,
    send_ref, proj_held, rows_held, live_ref, signs_ref,
    rows_buf, lengths_buf, perm_buf, sems,
):
    k = lax.axis_index("tp")
    core = lax.rem(k, 2)
    copies = [
        pltpu.make_async_copy(perm_ref, perm_buf, sems.at[0]),
        pltpu.make_async_copy(lengths_ref, lengths_buf, sems.at[1]),
        pltpu.make_async_copy(rows_ref.at[1 - core], rows_buf, sems.at[2]),
        pltpu.make_async_copy(proj_ref, proj_held, sems.at[3]),
        pltpu.make_async_copy(rows_ref.at[core], rows_held, sems.at[4]),
    ]
    for copy in copies:
        copy.start()
    copies[0].wait()
    copies[1].wait()
    position = lax.broadcasted_iota(jnp.int32, live_ref.shape, 1)
    live_ref[...] = (position < lengths_buf[core]).astype(jnp.float32)
    row = lax.broadcasted_iota(jnp.int32, signs_ref.shape, 0)
    source = lax.broadcasted_iota(jnp.int32, signs_ref.shape, 1)
    example = (source // 4) * 2 + source % 2
    signs = jnp.zeros(signs_ref.shape, jnp.float32)
    for slot in range(perm_ref.shape[0]):
        pair = slot // 2
        place = ((pair // pairs_mine) ^ k) * pairs_mine + pair % pairs_mine
        hit = (row == place) & (example == perm_buf[slot])
        signs = jnp.where(hit, 1.0 if slot % 2 else -1.0, signs)
    signs_ref[...] = signs
    copies[2].wait()
    copies[3].wait()
    put_factor(rows_buf[...], proj_held[...], send_ref, 0)
    copies[4].wait()


def out_send(proj, rows, lengths, pair_perm, sources, tp_count):
    rank, depth = proj.shape
    _, tokens, _ = rows.shape
    pair_count = pair_perm.shape[0] // 2
    return pl.pallas_call(
        functools.partial(out_send_kernel, pair_count // tp_count),
        out_shape=[
            jax.ShapeDtypeStruct((rank, tokens), jnp.float32),
            jax.ShapeDtypeStruct(proj.shape, proj.dtype),
            jax.ShapeDtypeStruct((tokens, depth), rows.dtype),
            jax.ShapeDtypeStruct((1, tokens), jnp.float32),
            jax.ShapeDtypeStruct((pair_count, sources), jnp.float32),
        ],
        in_specs=[ANY] * 4,
        out_specs=[VMEM] * 5,
        scratch_shapes=[
            pltpu.VMEM((tokens, depth), rows.dtype),
            pltpu.SMEM(lengths.shape, lengths.dtype),
            pltpu.SMEM(pair_perm.shape, pair_perm.dtype),
            pltpu.SemaphoreType.DMA((5,)),
        ],
        compiler_params=pltpu.CompilerParams(vmem_limit_bytes=8 << 20),
        cost_estimate=pl.CostEstimate(
            flops=4 * rank * depth * tokens, bytes_accessed=4 * depth * tokens, transcendentals=0
        ),
    )(in_hbm(proj), in_hbm(rows), in_hbm(lengths), in_hbm(pair_perm))


def out_keep_kernel(proj_ref, rows_ref, out_ref):
    put_factor(rows_ref[...], proj_ref[...], out_ref, 0)


def out_keep(proj, rows):
    rank, depth = proj.shape
    tokens, _ = rows.shape
    return pl.pallas_call(
        out_keep_kernel,
        out_shape=jax.ShapeDtypeStruct((rank, tokens), jnp.float32),
        in_specs=[VMEM, VMEM],
        out_specs=VMEM,
        compiler_params=pltpu.CompilerParams(vmem_limit_bytes=8 << 20),
        cost_estimate=pl.CostEstimate(
            flops=4 * 10**9, bytes_accessed=2 * depth * tokens, transcendentals=0
        ),
    )(proj, rows)


def add_kernel(left_ref, right_ref, out_ref):
    out_ref[...] = left_ref[...] + right_ref[...]


def add(left, right, flops):
    return pl.pallas_call(
        add_kernel,
        out_shape=jax.ShapeDtypeStruct(left.shape, left.dtype),
        in_specs=[VMEM, VMEM],
        out_specs=VMEM,
        compiler_params=pltpu.CompilerParams(vmem_limit_bytes=4 << 20),
        cost_estimate=pl.CostEstimate(flops=flops, bytes_accessed=16 << 20, transcendentals=0),
    )(left, right)


def in_kernel(proj_ref, rows_ref, after_ref, send_ref, keep_ref):
    core = lax.rem(lax.axis_index("tp"), 2)
    tokens = rows_ref.shape[1]
    for swap, out_ref in ((1, send_ref), (0, keep_ref)):
        prompt = lax.rem(core + swap, 2)
        for start in range(0, tokens, 256):
            put_factor(rows_ref[prompt, start : start + 256, :], proj_ref[...], out_ref, start)


def in_factors(proj, rows, after):
    rank, depth = proj.shape
    tokens = rows.shape[1]
    return pl.pallas_call(
        in_kernel,
        out_shape=[jax.ShapeDtypeStruct((rank, tokens), jnp.float32)] * 2,
        in_specs=[VMEM, VMEM, ANY],
        out_specs=[VMEM, VMEM],
        compiler_params=pltpu.CompilerParams(vmem_limit_bytes=8 << 20),
        cost_estimate=pl.CostEstimate(
            flops=8 * rank * depth * tokens, bytes_accessed=4 * depth * tokens, transcendentals=0
        ),
    )(proj, rows, after)


def outer_kernel(live_ref, in_keep_ref, in_got_ref, out_full_ref, after_ref, send_ref, grads_ref):
    rank = in_keep_ref.shape[0]
    masked = jnp.where(live_ref[...] > 0.0, in_keep_ref[...] + in_got_ref[...], 0.0)
    grads_ref[...] = lax.dot_general(
        masked,
        out_full_ref[...],
        (((1,), (1,)), ((), ())),
        precision=lax.Precision.HIGHEST,
        preferred_element_type=jnp.float32,
    )
    half = rank // 2
    even = grads_ref[pl.ds(0, half, stride=2), :]
    odd = grads_ref[pl.ds(1, half, stride=2), :]
    packed = jnp.concatenate([even, odd], axis=1)
    for target in range(send_ref.shape[0]):
        share = target % 4
        send_ref[target] = packed[share * 8 : share * 8 + 8, :]


def outer(live, in_keep, in_got, out_full, after, targets):
    rank, tokens = in_keep.shape
    return pl.pallas_call(
        outer_kernel,
        out_shape=jax.ShapeDtypeStruct((targets, rank // 8, 2 * rank), jnp.float32),
        in_specs=[VMEM] * 4 + [ANY],
        out_specs=VMEM,
        scratch_shapes=[pltpu.VMEM((rank, rank), jnp.float32)],
        compiler_params=pltpu.CompilerParams(vmem_limit_bytes=8 << 20),
        cost_estimate=pl.CostEstimate(
            flops=12 * rank * rank * tokens, bytes_accessed=4 * rank * tokens, transcendentals=0
        ),
    )(live, in_keep, in_got, out_full, after)


def norm_kernel(slab_ref, after_ref, out_ref):
    rows, cols = slab_ref.shape
    for start in range(0, rows, 128):
        total = jnp.zeros((128, 128), jnp.float32)
        for at in range(0, cols, 128):
            wide = slab_ref[start : start + 128, at : at + 128].astype(jnp.float32)
            total = total + wide * wide
        out_ref[:, start : start + 128] = jnp.sum(total.T, axis=0, keepdims=True)


def norms(slab, after):
    rows, cols = slab.shape
    return pl.pallas_call(
        norm_kernel,
        out_shape=jax.ShapeDtypeStruct((1, rows), jnp.float32),
        in_specs=[VMEM, ANY],
        out_specs=VMEM,
        compiler_params=pltpu.CompilerParams(vmem_limit_bytes=8 << 20),
        cost_estimate=pl.CostEstimate(
            flops=2 * rows * cols, bytes_accessed=2 * rows * cols, transcendentals=0
        ),
    )(slab, after)


def dots_kernel(signs_ref, partials_ref, slab_ref, norm_ref, *message_refs):
    pair_count = signs_ref.shape[0]
    pairs_mine = pair_count // len(message_refs)
    rows = slab_ref.shape[0]
    blocks = [partials_ref[:, r, :] for r in range(partials_ref.shape[1])]
    partials = jnp.concatenate(blocks, axis=1)
    queries = lax.dot_general(
        signs_ref[...],
        partials,
        (((1,), (0,)), ((), ())),
        precision=lax.Precision.HIGHEST,
        preferred_element_type=jnp.float32,
    )
    query_sq = jnp.sum(queries * queries, axis=1, keepdims=True)
    dots = lax.dot_general(
        queries.astype(jnp.bfloat16),
        slab_ref[...],
        (((1,), (1,)), ((), ())),
        preferred_element_type=jnp.float32,
    )
    for step, message_ref in enumerate(message_refs):
        mine = slice(step * pairs_mine, (step + 1) * pairs_mine)
        message_ref[0:pairs_mine, 0:rows] = dots[mine]
        message_ref[pairs_mine : pairs_mine + 1, 0:rows] = norm_ref[...]
        message_ref[0:pairs_mine, rows : rows + 128] = jnp.broadcast_to(query_sq[mine], (pairs_mine, 128))
        message_ref[pairs_mine : pairs_mine + 1, rows : rows + 128] = jnp.zeros((1, 128), jnp.float32)


def dots(signs, partials, slab, bank_part, tp_count):
    pair_count = signs.shape[0]
    rows, cols = slab.shape
    message = jax.ShapeDtypeStruct((pair_count // tp_count + 1, rows + 128), jnp.float32)
    return pl.pallas_call(
        dots_kernel,
        out_shape=[message] * tp_count,
        in_specs=[VMEM, VMEM, VMEM, VMEM],
        out_specs=[VMEM] * tp_count,
        compiler_params=pltpu.CompilerParams(vmem_limit_bytes=8 << 20),
        cost_estimate=pl.CostEstimate(
            flops=2 * pair_count * rows * cols, bytes_accessed=2 * rows * cols, transcendentals=0
        ),
    )(signs, partials, slab, bank_part)


def scores_kernel(scale, own_ref, *refs):
    *got_refs, out_ref = refs
    total = own_ref[...]
    for got_ref in got_refs:
        total = total + got_ref[...]
    pairs, rows = out_ref.shape
    bank_scale = lax.rsqrt(total[pairs : pairs + 1, 0:rows] + epsilon)
    query_scale = lax.rsqrt(total[0:pairs, rows : rows + 1] + epsilon)
    out_ref[...] = total[0:pairs, 0:rows] * scale * query_scale * bank_scale


def scores(messages, scale):
    pairs = messages[0].shape[0] - 1
    rows = messages[0].shape[1] - 128
    return pl.pallas_call(
        functools.partial(scores_kernel, scale),
        out_shape=jax.ShapeDtypeStruct((pairs, rows), jnp.float32),
        in_specs=[VMEM] * len(messages),
        out_specs=VMEM,
        compiler_params=pltpu.CompilerParams(vmem_limit_bytes=8 << 20),
    )(*messages)


def per_device(hidden, out_grad, proj_in, proj_out, lengths, pair_perm, bank_slab):
    rank = proj_in.shape[0]
    tp_count = lax.axis_size("tp")
    bank_count = lax.axis_size("bank")
    out_away, proj_held, rows_held, live, signs = out_send(
        proj_out, out_grad, lengths, pair_perm, bank_count * tp_count, tp_count
    )
    out_got = lax.ppermute(out_away, "tp", flip(1))
    out_chip = add(out_keep(proj_held, rows_held), out_got, 4)
    out_other = lax.ppermute(out_chip, "tp", flip(2))
    in_away, in_keep = in_factors(proj_in, hidden, out_chip)
    in_got = lax.ppermute(in_away, "tp", flip(1))
    out_full = add(out_chip, out_other, 4 * 10**9)
    bank_part = norms(bank_slab, in_away)
    outgoing = outer(live, in_keep, in_got, out_full, bank_part, bank_count * tp_count)
    partials = lax.all_to_all(outgoing, ("bank", "tp"), 0, 0, tiled=True)
    messages = dots(signs, partials, bank_slab, bank_part, tp_count)
    got = [messages[0]] + [lax.ppermute(messages[step], "tp", flip(step)) for step in range(1, 4)]
    return scores(got, float(rank))


def solution(mesh):
    return jax.shard_map(
        per_device,
        mesh=mesh,
        in_specs=(
            P("bank", None, "tp"),
            P("bank", None, "tp"),
            P(None, "tp"),
            P(None, "tp"),
            P("bank"),
            P(),
            P("bank", "tp"),
        ),
        out_specs=P("tp", "bank"),
        check_vma=False,
    )
```

```python
import functools

import jax
import jax.numpy as jnp
from jax import lax
from jax.experimental import pallas as pl
from jax.experimental.pallas import tpu as pltpu
from jax.sharding import PartitionSpec as P

epsilon = 1e-06
VMEM = pl.BlockSpec(memory_space=pltpu.VMEM)
ANY = pl.BlockSpec(memory_space=pl.ANY)


def flip(step):
    return [(i, i ^ step) for i in range(4)]


def exchange_order(bank_count):
    far = bank_count // 2
    return [
        ((far - 1 - high) * 2 + low) * 4 + chip * 2 + core
        for chip in range(2)
        for low in range(2)
        for core in range(2)
        for high in range(far)
    ]


def put_factor(rows, proj, out_ref, start):
    part = lax.dot_general(
        rows, proj, (((1,), (1,)), ((), ())), preferred_element_type=jnp.float32
    )
    out_ref[:, start : start + rows.shape[0]] = part.T


def in_hbm(arr):
    return pltpu.with_memory_space_constraint(arr, pltpu.HBM)


def out_send_kernel(
    pairs_mine, proj_ref, rows_ref, lengths_ref, perm_ref,
    send_ref, proj_held, rows_held, live_ref, signs_ref,
    rows_buf, lengths_buf, perm_buf, sems,
):
    k = lax.axis_index("tp")
    core = lax.rem(k, 2)
    copies = [
        pltpu.make_async_copy(perm_ref, perm_buf, sems.at[0]),
        pltpu.make_async_copy(lengths_ref, lengths_buf, sems.at[1]),
        pltpu.make_async_copy(rows_ref.at[1 - core], rows_buf, sems.at[2]),
        pltpu.make_async_copy(proj_ref, proj_held, sems.at[3]),
        pltpu.make_async_copy(rows_ref.at[core], rows_held, sems.at[4]),
    ]
    for copy in copies:
        copy.start()
    copies[0].wait()
    copies[1].wait()
    position = lax.broadcasted_iota(jnp.int32, live_ref.shape, 1)
    live_ref[...] = (position < lengths_buf[core]).astype(jnp.float32)
    row = lax.broadcasted_iota(jnp.int32, signs_ref.shape, 0)
    source = lax.broadcasted_iota(jnp.int32, signs_ref.shape, 1)
    far = signs_ref.shape[1] // 8
    bank = (far - 1 - source % far) * 2 + (source // (2 * far)) % 2
    example = bank * 2 + (source // far) % 2
    signs = jnp.zeros(signs_ref.shape, jnp.float32)
    for slot in range(perm_ref.shape[0]):
        pair = slot // 2
        place = ((pair // pairs_mine) ^ k) * pairs_mine + pair % pairs_mine
        hit = (row == place) & (example == perm_buf[slot])
        signs = jnp.where(hit, 1.0 if slot % 2 else -1.0, signs)
    signs_ref[...] = signs
    copies[2].wait()
    copies[3].wait()
    put_factor(rows_buf[...], proj_held[...], send_ref, 0)
    copies[4].wait()


def out_send(proj, rows, lengths, pair_perm, sources, tp_count):
    rank, depth = proj.shape
    _, tokens, _ = rows.shape
    pair_count = pair_perm.shape[0] // 2
    return pl.pallas_call(
        functools.partial(out_send_kernel, pair_count // tp_count),
        out_shape=[
            jax.ShapeDtypeStruct((rank, tokens), jnp.float32),
            jax.ShapeDtypeStruct(proj.shape, proj.dtype),
            jax.ShapeDtypeStruct((tokens, depth), rows.dtype),
            jax.ShapeDtypeStruct((1, tokens), jnp.float32),
            jax.ShapeDtypeStruct((pair_count, sources), jnp.float32),
        ],
        in_specs=[ANY] * 4,
        out_specs=[VMEM] * 5,
        scratch_shapes=[
            pltpu.VMEM((tokens, depth), rows.dtype),
            pltpu.SMEM(lengths.shape, lengths.dtype),
            pltpu.SMEM(pair_perm.shape, pair_perm.dtype),
            pltpu.SemaphoreType.DMA((5,)),
        ],
        compiler_params=pltpu.CompilerParams(vmem_limit_bytes=8 << 20),
        cost_estimate=pl.CostEstimate(
            flops=4 * rank * depth * tokens, bytes_accessed=4 * depth * tokens, transcendentals=0
        ),
    )(in_hbm(proj), in_hbm(rows), in_hbm(lengths), in_hbm(pair_perm))


def out_keep_kernel(proj_ref, rows_ref, out_ref):
    put_factor(rows_ref[...], proj_ref[...], out_ref, 0)


def out_keep(proj, rows):
    rank, depth = proj.shape
    tokens, _ = rows.shape
    return pl.pallas_call(
        out_keep_kernel,
        out_shape=jax.ShapeDtypeStruct((rank, tokens), jnp.float32),
        in_specs=[VMEM, VMEM],
        out_specs=VMEM,
        compiler_params=pltpu.CompilerParams(vmem_limit_bytes=8 << 20),
        cost_estimate=pl.CostEstimate(
            flops=4 * 10**9, bytes_accessed=2 * depth * tokens, transcendentals=0
        ),
    )(proj, rows)


def add_kernel(left_ref, right_ref, out_ref):
    out_ref[...] = left_ref[...] + right_ref[...]


def add(left, right, flops):
    return pl.pallas_call(
        add_kernel,
        out_shape=jax.ShapeDtypeStruct(left.shape, left.dtype),
        in_specs=[VMEM, VMEM],
        out_specs=VMEM,
        compiler_params=pltpu.CompilerParams(vmem_limit_bytes=4 << 20),
        cost_estimate=pl.CostEstimate(flops=flops, bytes_accessed=16 << 20, transcendentals=0),
    )(left, right)


def in_kernel(swap, proj_ref, rows_ref, after_ref, out_ref):
    prompt = lax.rem(lax.axis_index("tp") + swap, 2)
    tokens = rows_ref.shape[1]
    for start in range(0, tokens, 256):
        put_factor(rows_ref[prompt, start : start + 256, :], proj_ref[...], out_ref, start)


def in_factor(proj, rows, after, swap):
    rank, depth = proj.shape
    tokens = rows.shape[1]
    return pl.pallas_call(
        functools.partial(in_kernel, swap),
        out_shape=jax.ShapeDtypeStruct((rank, tokens), jnp.float32),
        in_specs=[VMEM, VMEM, ANY],
        out_specs=VMEM,
        compiler_params=pltpu.CompilerParams(vmem_limit_bytes=8 << 20),
        cost_estimate=pl.CostEstimate(
            flops=4 * rank * depth * tokens, bytes_accessed=2 * depth * tokens, transcendentals=0
        ),
    )(proj, rows, after)


def outer_kernel(shares, live_ref, in_keep_ref, in_got_ref, out_full_ref, after_ref, send_ref, grads_ref):
    rank = in_keep_ref.shape[0]
    masked = jnp.where(live_ref[...] > 0.0, in_keep_ref[...] + in_got_ref[...], 0.0)
    grads_ref[...] = lax.dot_general(
        masked,
        out_full_ref[...],
        (((1,), (1,)), ((), ())),
        precision=lax.Precision.HIGHEST,
        preferred_element_type=jnp.float32,
    )
    half = rank // 2
    even = grads_ref[pl.ds(0, half, stride=2), :]
    odd = grads_ref[pl.ds(1, half, stride=2), :]
    packed = jnp.concatenate([even, odd], axis=1)
    for target, share in enumerate(shares):
        send_ref[target] = packed[share * 8 : share * 8 + 8, :]


def outer(live, in_keep, in_got, out_full, after, shares):
    rank, tokens = in_keep.shape
    return pl.pallas_call(
        functools.partial(outer_kernel, shares),
        out_shape=jax.ShapeDtypeStruct((len(shares), rank // 8, 2 * rank), jnp.float32),
        in_specs=[VMEM] * 4 + [ANY],
        out_specs=VMEM,
        scratch_shapes=[pltpu.VMEM((rank, rank), jnp.float32)],
        compiler_params=pltpu.CompilerParams(vmem_limit_bytes=8 << 20),
        cost_estimate=pl.CostEstimate(
            flops=12 * rank * rank * tokens, bytes_accessed=4 * rank * tokens, transcendentals=0
        ),
    )(live, in_keep, in_got, out_full, after)


def norm_kernel(slab_ref, after_ref, out_ref):
    rows, cols = slab_ref.shape
    for start in range(0, rows, 128):
        total = jnp.zeros((128, 128), jnp.float32)
        for at in range(0, cols, 128):
            wide = slab_ref[start : start + 128, at : at + 128].astype(jnp.float32)
            total = total + wide * wide
        out_ref[:, start : start + 128] = jnp.sum(total.T, axis=0, keepdims=True)


def norms(slab, after):
    rows, cols = slab.shape
    return pl.pallas_call(
        norm_kernel,
        out_shape=jax.ShapeDtypeStruct((1, rows), jnp.float32),
        in_specs=[VMEM, ANY],
        out_specs=VMEM,
        compiler_params=pltpu.CompilerParams(vmem_limit_bytes=8 << 20),
        cost_estimate=pl.CostEstimate(
            flops=2 * rows * cols, bytes_accessed=2 * rows * cols, transcendentals=0
        ),
    )(slab, after)


def norm_chunk(rows, pairs_mine):
    return max(128, rows // pairs_mine)


def dots_kernel(signs_ref, partials_ref, slab_ref, norm_ref, *message_refs):
    pair_count = signs_ref.shape[0]
    pairs_mine = pair_count // len(message_refs)
    rows = slab_ref.shape[0]
    blocks = [partials_ref[:, r, :] for r in range(partials_ref.shape[1])]
    partials = jnp.concatenate(blocks, axis=1)
    queries = lax.dot_general(
        signs_ref[...],
        partials,
        (((1,), (0,)), ((), ())),
        precision=lax.Precision.HIGHEST,
        preferred_element_type=jnp.float32,
    )
    query_sq = jnp.sum(queries * queries, axis=1, keepdims=True)
    dots = lax.dot_general(
        queries.astype(jnp.bfloat16),
        slab_ref[...],
        (((1,), (1,)), ((), ())),
        preferred_element_type=jnp.float32,
    )
    chunk = norm_chunk(rows, pairs_mine)
    for step, message_ref in enumerate(message_refs):
        mine = slice(step * pairs_mine, (step + 1) * pairs_mine)
        message_ref[:, 0:rows] = dots[mine]
        message_ref[:, rows : rows + chunk] = jnp.zeros((pairs_mine, chunk), jnp.float32)
        for row in range(rows // chunk):
            message_ref[row : row + 1, rows : rows + chunk] = norm_ref[:, row * chunk : (row + 1) * chunk]
        message_ref[:, rows + chunk :] = jnp.broadcast_to(query_sq[mine], (pairs_mine, 128))


def dots(signs, partials, slab, bank_part, tp_count):
    pair_count = signs.shape[0]
    rows, cols = slab.shape
    pairs_mine = pair_count // tp_count
    message = jax.ShapeDtypeStruct(
        (pairs_mine, rows + norm_chunk(rows, pairs_mine) + 128), jnp.float32
    )
    return pl.pallas_call(
        dots_kernel,
        out_shape=[message] * tp_count,
        in_specs=[VMEM, VMEM, VMEM, VMEM],
        out_specs=[VMEM] * tp_count,
        compiler_params=pltpu.CompilerParams(vmem_limit_bytes=8 << 20),
        cost_estimate=pl.CostEstimate(
            flops=2 * pair_count * rows * cols, bytes_accessed=2 * rows * cols, transcendentals=0
        ),
    )(signs, partials, slab, bank_part)


def scores_kernel(scale, own_ref, *refs):
    *got_refs, out_ref = refs
    total = own_ref[...]
    for got_ref in got_refs:
        total = total + got_ref[...]
    pairs, rows = out_ref.shape
    chunk = norm_chunk(rows, pairs)
    query_scale = scale * lax.rsqrt(total[:, rows + chunk : rows + chunk + 1] + epsilon)
    bank_scale = lax.rsqrt(total[:, rows : rows + chunk] + epsilon)
    for row in range(rows // chunk):
        span = slice(row * chunk, (row + 1) * chunk)
        out_ref[:, span] = total[:, span] * query_scale * bank_scale[row : row + 1, :]


def scores(messages, rows, scale):
    pairs = messages[0].shape[0]
    return pl.pallas_call(
        functools.partial(scores_kernel, scale),
        out_shape=jax.ShapeDtypeStruct((pairs, rows), jnp.float32),
        in_specs=[VMEM] * len(messages),
        out_specs=VMEM,
        compiler_params=pltpu.CompilerParams(vmem_limit_bytes=8 << 20),
    )(*messages)


def per_device(hidden, out_grad, proj_in, proj_out, lengths, pair_perm, bank_slab):
    rank = proj_in.shape[0]
    tp_count = lax.axis_size("tp")
    bank_count = lax.axis_size("bank")
    out_away, proj_held, rows_held, live, signs = out_send(
        proj_out, out_grad, lengths, pair_perm, bank_count * tp_count, tp_count
    )
    out_got = lax.ppermute(out_away, "tp", flip(1))
    out_chip = add(out_keep(proj_held, rows_held), out_got, 4)
    out_other = lax.ppermute(out_chip, "tp", flip(2))
    in_away = in_factor(proj_in, hidden, out_chip, 1)
    in_keep = in_factor(proj_in, hidden, in_away, 0)
    in_got = lax.ppermute(in_away, "tp", flip(1))
    out_full = add(out_chip, out_other, 4 * 10**9)
    bank_part = norms(bank_slab, in_away)
    outgoing = outer(
        live, in_keep, in_got, out_full, bank_part, [device % 4 for device in exchange_order(bank_count)]
    )
    partials = lax.all_to_all(
        outgoing, ("bank", "tp"), 0, 0, tiled=True, axis_index_groups=[exchange_order(bank_count)]
    )
    messages = dots(signs, partials, bank_slab, bank_part, tp_count)
    got = [messages[0]] + [lax.ppermute(messages[step], "tp", flip(step)) for step in (2, 3, 1)]
    return scores(got, bank_slab.shape[0], float(rank))


def solution(mesh):
    return jax.shard_map(
        per_device,
        mesh=mesh,
        in_specs=(
            P("bank", None, "tp"),
            P("bank", None, "tp"),
            P(None, "tp"),
            P(None, "tp"),
            P("bank"),
            P(),
            P("bank", "tp"),
        ),
        out_specs=P("tp", "bank"),
        check_vma=False,
    )
```

```python
import functools

import jax
import jax.numpy as jnp
from jax import lax
from jax.experimental import pallas as pl
from jax.experimental.pallas import tpu as pltpu
from jax.sharding import PartitionSpec as P

epsilon = 1e-06
VMEM = pl.BlockSpec(memory_space=pltpu.VMEM)
ANY = pl.BlockSpec(memory_space=pl.ANY)


def flip(step):
    return [(i, i ^ step) for i in range(4)]


def exchange_order(bank_count):
    far = bank_count // 2
    return [
        ((far - 1 - high) * 2 + low) * 4 + chip * 2 + core
        for chip in range(2)
        for low in range(2)
        for core in range(2)
        for high in range(far)
    ]


def put_factor(rows, proj, out_ref, start):
    part = lax.dot_general(
        rows, proj, (((1,), (1,)), ((), ())), preferred_element_type=jnp.float32
    )
    out_ref[:, start : start + rows.shape[0]] = part.T


def put_factor_rows(rows, proj, out_ref):
    out_ref[...] = lax.dot_general(
        proj, rows, (((1,), (1,)), ((), ())), preferred_element_type=jnp.float32
    )


def in_hbm(arr):
    return pltpu.with_memory_space_constraint(arr, pltpu.HBM)


def out_send_kernel(
    pairs_mine, proj_ref, rows_ref, lengths_ref, perm_ref,
    send_ref, proj_held, rows_held, live_ref, signs_ref,
    rows_buf, lengths_buf, perm_buf, sems,
):
    k = lax.axis_index("tp")
    core = lax.rem(k, 2)
    copies = [
        pltpu.make_async_copy(perm_ref, perm_buf, sems.at[0]),
        pltpu.make_async_copy(lengths_ref, lengths_buf, sems.at[1]),
        pltpu.make_async_copy(rows_ref.at[1 - core], rows_buf, sems.at[2]),
        pltpu.make_async_copy(proj_ref, proj_held, sems.at[3]),
        pltpu.make_async_copy(rows_ref.at[core], rows_held, sems.at[4]),
    ]
    for at, copy in enumerate(copies):
        copy.start(priority=1 if at == 4 else 0)
    copies[0].wait()
    copies[1].wait()
    position = lax.broadcasted_iota(jnp.int32, live_ref.shape, 1)
    live_ref[...] = (position < lengths_buf[core]).astype(jnp.float32)
    row = lax.broadcasted_iota(jnp.int32, signs_ref.shape, 0)
    source = lax.broadcasted_iota(jnp.int32, signs_ref.shape, 1)
    far = signs_ref.shape[1] // 8
    bank = (far - 1 - source % far) * 2 + (source // (2 * far)) % 2
    example = bank * 2 + (source // far) % 2
    signs = jnp.zeros(signs_ref.shape, jnp.float32)
    for slot in range(perm_ref.shape[0]):
        pair = slot // 2
        place = ((pair // pairs_mine) ^ k) * pairs_mine + pair % pairs_mine
        hit = (row == place) & (example == perm_buf[slot])
        signs = jnp.where(hit, 1.0 if slot % 2 else -1.0, signs)
    signs_ref[...] = signs
    copies[2].wait()
    copies[3].wait()
    put_factor_rows(rows_buf[...], proj_held[...], send_ref)
    copies[4].wait()


def out_send(proj, rows, lengths, pair_perm, sources, tp_count):
    rank, depth = proj.shape
    _, tokens, _ = rows.shape
    pair_count = pair_perm.shape[0] // 2
    return pl.pallas_call(
        functools.partial(out_send_kernel, pair_count // tp_count),
        out_shape=[
            jax.ShapeDtypeStruct((rank, tokens), jnp.float32),
            jax.ShapeDtypeStruct(proj.shape, proj.dtype),
            jax.ShapeDtypeStruct((tokens, depth), rows.dtype),
            jax.ShapeDtypeStruct((1, tokens), jnp.float32),
            jax.ShapeDtypeStruct((pair_count, sources), jnp.float32),
        ],
        in_specs=[ANY] * 4,
        out_specs=[VMEM] * 5,
        scratch_shapes=[
            pltpu.VMEM((tokens, depth), rows.dtype),
            pltpu.SMEM(lengths.shape, lengths.dtype),
            pltpu.SMEM(pair_perm.shape, pair_perm.dtype),
            pltpu.SemaphoreType.DMA((5,)),
        ],
        compiler_params=pltpu.CompilerParams(vmem_limit_bytes=8 << 20),
        cost_estimate=pl.CostEstimate(
            flops=4 * rank * depth * tokens, bytes_accessed=4 * depth * tokens, transcendentals=0
        ),
    )(in_hbm(proj), in_hbm(rows), in_hbm(lengths), in_hbm(pair_perm))


def out_keep_kernel(proj_ref, rows_ref, out_ref):
    put_factor_rows(rows_ref[...], proj_ref[...], out_ref)


def out_keep(proj, rows):
    rank, depth = proj.shape
    tokens, _ = rows.shape
    return pl.pallas_call(
        out_keep_kernel,
        out_shape=jax.ShapeDtypeStruct((rank, tokens), jnp.float32),
        in_specs=[VMEM, VMEM],
        out_specs=VMEM,
        compiler_params=pltpu.CompilerParams(vmem_limit_bytes=8 << 20),
        cost_estimate=pl.CostEstimate(
            flops=4 * 10**9, bytes_accessed=2 * depth * tokens, transcendentals=0
        ),
    )(proj, rows)


def add_kernel(left_ref, right_ref, out_ref):
    out_ref[...] = left_ref[...] + right_ref[...]


def add(left, right, flops):
    return pl.pallas_call(
        add_kernel,
        out_shape=jax.ShapeDtypeStruct(left.shape, left.dtype),
        in_specs=[VMEM, VMEM],
        out_specs=VMEM,
        compiler_params=pltpu.CompilerParams(vmem_limit_bytes=4 << 20),
        cost_estimate=pl.CostEstimate(flops=flops, bytes_accessed=16 << 20, transcendentals=0),
    )(left, right)


def in_kernel(swap, proj_ref, rows_ref, after_ref, out_ref):
    prompt = lax.rem(lax.axis_index("tp") + swap, 2)
    tokens = rows_ref.shape[1]
    for start in range(0, tokens, 256):
        put_factor(rows_ref[prompt, start : start + 256, :], proj_ref[...], out_ref, start)


def in_factor(proj, rows, after, swap):
    rank, depth = proj.shape
    tokens = rows.shape[1]
    return pl.pallas_call(
        functools.partial(in_kernel, swap),
        out_shape=jax.ShapeDtypeStruct((rank, tokens), jnp.float32),
        in_specs=[VMEM, VMEM, ANY],
        out_specs=VMEM,
        compiler_params=pltpu.CompilerParams(vmem_limit_bytes=8 << 20),
        cost_estimate=pl.CostEstimate(
            flops=4 * rank * depth * tokens, bytes_accessed=2 * depth * tokens, transcendentals=0
        ),
    )(proj, rows, after)


def halves(wide):
    high = wide.astype(jnp.bfloat16)
    return high, (wide - high.astype(jnp.float32)).astype(jnp.bfloat16)


def outer_kernel(shares, live_ref, in_keep_ref, in_got_ref, out_full_ref, after_ref, send_ref, grads_ref):
    rank = in_keep_ref.shape[0]
    masked = jnp.where(live_ref[...] > 0.0, in_keep_ref[...] + in_got_ref[...], 0.0)
    in_high, in_low = halves(masked)
    out_high, out_low = halves(out_full_ref[...])
    grads_ref[...] = lax.dot_general(
        jnp.concatenate([in_high, in_high, in_low], axis=1),
        jnp.concatenate([out_high, out_low, out_high], axis=1),
        (((1,), (1,)), ((), ())),
        preferred_element_type=jnp.float32,
    )
    half = rank // 2
    even = grads_ref[pl.ds(0, half, stride=2), :]
    odd = grads_ref[pl.ds(1, half, stride=2), :]
    packed = jnp.concatenate([even, odd], axis=1)
    for target, share in enumerate(shares):
        send_ref[target] = packed[share * 8 : share * 8 + 8, :]


def outer(live, in_keep, in_got, out_full, after, shares):
    rank, tokens = in_keep.shape
    return pl.pallas_call(
        functools.partial(outer_kernel, shares),
        out_shape=jax.ShapeDtypeStruct((len(shares), rank // 8, 2 * rank), jnp.float32),
        in_specs=[VMEM] * 4 + [ANY],
        out_specs=VMEM,
        scratch_shapes=[pltpu.VMEM((rank, rank), jnp.float32)],
        compiler_params=pltpu.CompilerParams(vmem_limit_bytes=8 << 20),
        cost_estimate=pl.CostEstimate(
            flops=12 * rank * rank * tokens, bytes_accessed=4 * rank * tokens, transcendentals=0
        ),
    )(live, in_keep, in_got, out_full, after)


def norm_kernel(slab_ref, after_ref, out_ref):
    rows, cols = slab_ref.shape
    for start in range(0, rows, 128):
        total = jnp.zeros((128, 128), jnp.float32)
        for at in range(0, cols, 128):
            wide = slab_ref[start : start + 128, at : at + 128].astype(jnp.float32)
            total = total + wide * wide
        out_ref[:, start : start + 128] = jnp.sum(total.T, axis=0, keepdims=True)


def norms(slab, after):
    rows, cols = slab.shape
    return pl.pallas_call(
        norm_kernel,
        out_shape=jax.ShapeDtypeStruct((1, rows), jnp.float32),
        in_specs=[VMEM, ANY],
        out_specs=VMEM,
        compiler_params=pltpu.CompilerParams(vmem_limit_bytes=8 << 20),
        cost_estimate=pl.CostEstimate(
            flops=2 * rows * cols, bytes_accessed=2 * rows * cols, transcendentals=0
        ),
    )(slab, after)


def norm_chunk(rows, pairs_mine):
    return max(128, rows // pairs_mine)


def dots_kernel(signs_ref, partials_ref, slab_ref, norm_ref, *message_refs):
    pair_count = signs_ref.shape[0]
    pairs_mine = pair_count // len(message_refs)
    rows = slab_ref.shape[0]
    blocks = [partials_ref[:, r, :] for r in range(partials_ref.shape[1])]
    partials = jnp.concatenate(blocks, axis=1)
    queries = lax.dot_general(
        signs_ref[...],
        partials,
        (((1,), (0,)), ((), ())),
        precision=lax.Precision.HIGHEST,
        preferred_element_type=jnp.float32,
    )
    query_sq = jnp.sum(queries * queries, axis=1, keepdims=True)
    dots = lax.dot_general(
        queries.astype(jnp.bfloat16),
        slab_ref[...],
        (((1,), (1,)), ((), ())),
        preferred_element_type=jnp.float32,
    )
    chunk = norm_chunk(rows, pairs_mine)
    for step, message_ref in enumerate(message_refs):
        mine = slice(step * pairs_mine, (step + 1) * pairs_mine)
        message_ref[:, 0:rows] = dots[mine]
        message_ref[:, rows : rows + chunk] = jnp.zeros((pairs_mine, chunk), jnp.float32)
        for row in range(rows // chunk):
            message_ref[row : row + 1, rows : rows + chunk] = norm_ref[:, row * chunk : (row + 1) * chunk]
        message_ref[:, rows + chunk :] = jnp.broadcast_to(query_sq[mine], (pairs_mine, 128))


def dots(signs, partials, slab, bank_part, tp_count):
    pair_count = signs.shape[0]
    rows, cols = slab.shape
    pairs_mine = pair_count // tp_count
    message = jax.ShapeDtypeStruct(
        (pairs_mine, rows + norm_chunk(rows, pairs_mine) + 128), jnp.float32
    )
    return pl.pallas_call(
        dots_kernel,
        out_shape=[message] * tp_count,
        in_specs=[VMEM, VMEM, VMEM, VMEM],
        out_specs=[VMEM] * tp_count,
        compiler_params=pltpu.CompilerParams(vmem_limit_bytes=8 << 20),
        cost_estimate=pl.CostEstimate(
            flops=2 * pair_count * rows * cols, bytes_accessed=2 * rows * cols, transcendentals=0
        ),
    )(signs, partials, slab, bank_part)


def scores_kernel(scale, own_ref, *refs):
    *got_refs, out_ref = refs
    total = own_ref[...]
    for got_ref in got_refs:
        total = total + got_ref[...]
    pairs, rows = out_ref.shape
    chunk = norm_chunk(rows, pairs)
    query_scale = scale * lax.rsqrt(total[:, rows + chunk : rows + chunk + 1] + epsilon)
    bank_scale = lax.rsqrt(total[:, rows : rows + chunk] + epsilon)
    for row in range(rows // chunk):
        span = slice(row * chunk, (row + 1) * chunk)
        out_ref[:, span] = total[:, span] * query_scale * bank_scale[row : row + 1, :]


def scores(messages, rows, scale):
    pairs = messages[0].shape[0]
    return pl.pallas_call(
        functools.partial(scores_kernel, scale),
        out_shape=jax.ShapeDtypeStruct((pairs, rows), jnp.float32),
        in_specs=[VMEM] * len(messages),
        out_specs=VMEM,
        compiler_params=pltpu.CompilerParams(vmem_limit_bytes=8 << 20),
    )(*messages)


def per_device(hidden, out_grad, proj_in, proj_out, lengths, pair_perm, bank_slab):
    rank = proj_in.shape[0]
    tp_count = lax.axis_size("tp")
    bank_count = lax.axis_size("bank")
    out_away, proj_held, rows_held, live, signs = out_send(
        proj_out, out_grad, lengths, pair_perm, bank_count * tp_count, tp_count
    )
    out_got = lax.ppermute(out_away, "tp", flip(1))
    out_chip = add(out_keep(proj_held, rows_held), out_got, 4)
    out_other = lax.ppermute(out_chip, "tp", flip(2))
    in_away = in_factor(proj_in, hidden, out_chip, 1)
    in_keep = in_factor(proj_in, hidden, in_away, 0)
    in_got = lax.ppermute(in_away, "tp", flip(1))
    out_full = add(out_chip, out_other, 4 * 10**9)
    bank_part = norms(bank_slab, in_away)
    outgoing = outer(
        live, in_keep, in_got, out_full, bank_part, [device % 4 for device in exchange_order(bank_count)]
    )
    partials = lax.all_to_all(
        outgoing, ("bank", "tp"), 0, 0, tiled=True, axis_index_groups=[exchange_order(bank_count)]
    )
    messages = dots(signs, partials, bank_slab, bank_part, tp_count)
    got = [messages[0]] + [lax.ppermute(messages[step], "tp", flip(step)) for step in (2, 3, 1)]
    return scores(got, bank_slab.shape[0], float(rank))


def solution(mesh):
    return jax.shard_map(
        per_device,
        mesh=mesh,
        in_specs=(
            P("bank", None, "tp"),
            P("bank", None, "tp"),
            P(None, "tp"),
            P(None, "tp"),
            P("bank"),
            P(),
            P("bank", "tp"),
        ),
        out_specs=P("tp", "bank"),
        check_vma=False,
    )
```

```python
import functools

import jax
import jax.numpy as jnp
from jax import lax
from jax.experimental import pallas as pl
from jax.experimental.pallas import tpu as pltpu
from jax.sharding import PartitionSpec as P

epsilon = 1e-06
VMEM = pl.BlockSpec(memory_space=pltpu.VMEM)
ANY = pl.BlockSpec(memory_space=pl.ANY)


def flip(step):
    return [(i, i ^ step) for i in range(4)]


def exchange_order(bank_count):
    far = bank_count // 2
    return [
        ((far - 1 - high) * 2 + low) * 4 + chip * 2 + core
        for chip in range(2)
        for low in range(2)
        for core in range(2)
        for high in range(far)
    ]


def put_factor(rows, proj, out_ref, start):
    part = lax.dot_general(
        rows, proj, (((1,), (1,)), ((), ())), preferred_element_type=jnp.float32
    )
    out_ref[:, start : start + rows.shape[0]] = part.T


def put_factor_rows(rows, proj, out_ref):
    out_ref[...] = lax.dot_general(
        proj, rows, (((1,), (1,)), ((), ())), preferred_element_type=jnp.float32
    )


def in_hbm(arr):
    return pltpu.with_memory_space_constraint(arr, pltpu.HBM)


def out_send_kernel(
    pairs_mine, proj_ref, rows_ref, lengths_ref, perm_ref,
    send_ref, proj_held, rows_held, live_ref, signs_ref,
    rows_buf, lengths_buf, perm_buf, sems,
):
    k = lax.axis_index("tp")
    core = lax.rem(k, 2)
    copies = [
        pltpu.make_async_copy(perm_ref, perm_buf, sems.at[0]),
        pltpu.make_async_copy(lengths_ref, lengths_buf, sems.at[1]),
        pltpu.make_async_copy(rows_ref.at[1 - core], rows_buf, sems.at[2]),
        pltpu.make_async_copy(proj_ref, proj_held, sems.at[3]),
        pltpu.make_async_copy(rows_ref.at[core], rows_held, sems.at[4]),
    ]
    for at in (2, 3, 0, 1, 4):
        copies[at].start(priority=1 if at == 4 else 0)
    copies[0].wait()
    copies[1].wait()
    position = lax.broadcasted_iota(jnp.int32, live_ref.shape, 1)
    live_ref[...] = (position < lengths_buf[core]).astype(jnp.float32)
    row = lax.broadcasted_iota(jnp.int32, signs_ref.shape, 0)
    source = lax.broadcasted_iota(jnp.int32, signs_ref.shape, 1)
    far = signs_ref.shape[1] // 8
    bank = (far - 1 - source % far) * 2 + (source // (2 * far)) % 2
    example = bank * 2 + (source // far) % 2
    signs = jnp.zeros(signs_ref.shape, jnp.float32)
    for slot in range(perm_ref.shape[0]):
        pair = slot // 2
        place = ((pair // pairs_mine) ^ k) * pairs_mine + pair % pairs_mine
        hit = (row == place) & (example == perm_buf[slot])
        signs = jnp.where(hit, 1.0 if slot % 2 else -1.0, signs)
    signs_ref[...] = signs
    copies[2].wait()
    copies[3].wait()
    put_factor_rows(rows_buf[...], proj_held[...], send_ref)
    copies[4].wait()


def out_send(proj, rows, lengths, pair_perm, sources, tp_count):
    rank, depth = proj.shape
    _, tokens, _ = rows.shape
    pair_count = pair_perm.shape[0] // 2
    return pl.pallas_call(
        functools.partial(out_send_kernel, pair_count // tp_count),
        out_shape=[
            jax.ShapeDtypeStruct((rank, tokens), jnp.float32),
            jax.ShapeDtypeStruct(proj.shape, proj.dtype),
            jax.ShapeDtypeStruct((tokens, depth), rows.dtype),
            jax.ShapeDtypeStruct((1, tokens), jnp.float32),
            jax.ShapeDtypeStruct((pair_count, sources), jnp.float32),
        ],
        in_specs=[ANY] * 4,
        out_specs=[VMEM] * 5,
        scratch_shapes=[
            pltpu.VMEM((tokens, depth), rows.dtype),
            pltpu.SMEM(lengths.shape, lengths.dtype),
            pltpu.SMEM(pair_perm.shape, pair_perm.dtype),
            pltpu.SemaphoreType.DMA((5,)),
        ],
        compiler_params=pltpu.CompilerParams(vmem_limit_bytes=8 << 20),
        cost_estimate=pl.CostEstimate(
            flops=4 * rank * depth * tokens, bytes_accessed=4 * depth * tokens, transcendentals=0
        ),
    )(in_hbm(proj), in_hbm(rows), in_hbm(lengths), in_hbm(pair_perm))


def out_keep_kernel(proj_ref, rows_ref, out_ref):
    put_factor_rows(rows_ref[...], proj_ref[...], out_ref)


def out_keep(proj, rows):
    rank, depth = proj.shape
    tokens, _ = rows.shape
    return pl.pallas_call(
        out_keep_kernel,
        out_shape=jax.ShapeDtypeStruct((rank, tokens), jnp.float32),
        in_specs=[VMEM, VMEM],
        out_specs=VMEM,
        compiler_params=pltpu.CompilerParams(vmem_limit_bytes=8 << 20),
        cost_estimate=pl.CostEstimate(
            flops=4 * 10**9, bytes_accessed=2 * depth * tokens, transcendentals=0
        ),
    )(proj, rows)


def add_kernel(left_ref, right_ref, out_ref):
    out_ref[...] = left_ref[...] + right_ref[...]


def add(left, right, flops):
    return pl.pallas_call(
        add_kernel,
        out_shape=jax.ShapeDtypeStruct(left.shape, left.dtype),
        in_specs=[VMEM, VMEM],
        out_specs=VMEM,
        compiler_params=pltpu.CompilerParams(vmem_limit_bytes=4 << 20),
        cost_estimate=pl.CostEstimate(flops=flops, bytes_accessed=16 << 20, transcendentals=0),
    )(left, right)


def in_kernel(swap, proj_ref, rows_ref, after_ref, out_ref):
    prompt = lax.rem(lax.axis_index("tp") + swap, 2)
    tokens = rows_ref.shape[1]
    for start in range(0, tokens, 256):
        put_factor(rows_ref[prompt, start : start + 256, :], proj_ref[...], out_ref, start)


def in_factor(proj, rows, after, swap):
    rank, depth = proj.shape
    tokens = rows.shape[1]
    return pl.pallas_call(
        functools.partial(in_kernel, swap),
        out_shape=jax.ShapeDtypeStruct((rank, tokens), jnp.float32),
        in_specs=[VMEM, VMEM, ANY],
        out_specs=VMEM,
        compiler_params=pltpu.CompilerParams(vmem_limit_bytes=8 << 20),
        cost_estimate=pl.CostEstimate(
            flops=4 * rank * depth * tokens, bytes_accessed=2 * depth * tokens, transcendentals=0
        ),
    )(proj, rows, after)


def halves(wide):
    high = wide.astype(jnp.bfloat16)
    return high, (wide - high.astype(jnp.float32)).astype(jnp.bfloat16)


def outer_kernel(shares, live_ref, in_keep_ref, in_got_ref, out_full_ref, after_ref, send_ref, grads_ref):
    rank = in_keep_ref.shape[0]
    masked = jnp.where(live_ref[...] > 0.0, in_keep_ref[...] + in_got_ref[...], 0.0)
    in_high, in_low = halves(masked)
    out_high, out_low = halves(out_full_ref[...])
    grads_ref[...] = lax.dot_general(
        jnp.concatenate([in_high, in_high, in_low], axis=1),
        jnp.concatenate([out_high, out_low, out_high], axis=1),
        (((1,), (1,)), ((), ())),
        preferred_element_type=jnp.float32,
    )
    half = rank // 2
    even = grads_ref[pl.ds(0, half, stride=2), :]
    odd = grads_ref[pl.ds(1, half, stride=2), :]
    packed = jnp.concatenate([even, odd], axis=1)
    for target, share in enumerate(shares):
        send_ref[target] = packed[share * 8 : share * 8 + 8, :]


def outer(live, in_keep, in_got, out_full, after, shares):
    rank, tokens = in_keep.shape
    return pl.pallas_call(
        functools.partial(outer_kernel, shares),
        out_shape=jax.ShapeDtypeStruct((len(shares), rank // 8, 2 * rank), jnp.float32),
        in_specs=[VMEM] * 4 + [ANY],
        out_specs=VMEM,
        scratch_shapes=[pltpu.VMEM((rank, rank), jnp.float32)],
        compiler_params=pltpu.CompilerParams(vmem_limit_bytes=8 << 20),
        cost_estimate=pl.CostEstimate(
            flops=12 * rank * rank * tokens, bytes_accessed=4 * rank * tokens, transcendentals=0
        ),
    )(live, in_keep, in_got, out_full, after)


def norm_kernel(slab_ref, after_ref, out_ref):
    rows, cols = slab_ref.shape
    for start in range(0, rows, 128):
        total = jnp.zeros((128, 128), jnp.float32)
        for at in range(0, cols, 128):
            wide = slab_ref[start : start + 128, at : at + 128].astype(jnp.float32)
            total = total + wide * wide
        out_ref[:, start : start + 128] = jnp.sum(total.T, axis=0, keepdims=True)


def norms(slab, after):
    rows, cols = slab.shape
    return pl.pallas_call(
        norm_kernel,
        out_shape=jax.ShapeDtypeStruct((1, rows), jnp.float32),
        in_specs=[VMEM, ANY],
        out_specs=VMEM,
        compiler_params=pltpu.CompilerParams(vmem_limit_bytes=8 << 20),
        cost_estimate=pl.CostEstimate(
            flops=2 * rows * cols, bytes_accessed=2 * rows * cols, transcendentals=0
        ),
    )(slab, after)


def norm_chunk(rows, pairs_mine):
    return max(128, rows // pairs_mine)


def dots_kernel(signs_ref, partials_ref, slab_ref, norm_ref, *message_refs):
    pair_count = signs_ref.shape[0]
    pairs_mine = pair_count // len(message_refs)
    rows = slab_ref.shape[0]
    blocks = [partials_ref[:, r, :] for r in range(partials_ref.shape[1])]
    partials = jnp.concatenate(blocks, axis=1)
    queries = lax.dot_general(
        signs_ref[...],
        partials,
        (((1,), (0,)), ((), ())),
        precision=lax.Precision.HIGHEST,
        preferred_element_type=jnp.float32,
    )
    query_sq = jnp.sum(queries * queries, axis=1, keepdims=True)
    dots = lax.dot_general(
        queries.astype(jnp.bfloat16),
        slab_ref[...],
        (((1,), (1,)), ((), ())),
        preferred_element_type=jnp.float32,
    )
    chunk = norm_chunk(rows, pairs_mine)
    for step, message_ref in enumerate(message_refs):
        mine = slice(step * pairs_mine, (step + 1) * pairs_mine)
        message_ref[:, 0:rows] = dots[mine]
        message_ref[:, rows : rows + chunk] = jnp.zeros((pairs_mine, chunk), jnp.float32)
        for row in range(rows // chunk):
            message_ref[row : row + 1, rows : rows + chunk] = norm_ref[:, row * chunk : (row + 1) * chunk]
        message_ref[:, rows + chunk :] = jnp.broadcast_to(query_sq[mine], (pairs_mine, 128))


def dots(signs, partials, slab, bank_part, tp_count):
    pair_count = signs.shape[0]
    rows, cols = slab.shape
    pairs_mine = pair_count // tp_count
    message = jax.ShapeDtypeStruct(
        (pairs_mine, rows + norm_chunk(rows, pairs_mine) + 128), jnp.float32
    )
    return pl.pallas_call(
        dots_kernel,
        out_shape=[message] * tp_count,
        in_specs=[VMEM, VMEM, VMEM, VMEM],
        out_specs=[VMEM] * tp_count,
        compiler_params=pltpu.CompilerParams(vmem_limit_bytes=8 << 20),
        cost_estimate=pl.CostEstimate(
            flops=2 * pair_count * rows * cols, bytes_accessed=2 * rows * cols, transcendentals=0
        ),
    )(signs, partials, slab, bank_part)


def scores_kernel(scale, own_ref, *refs):
    *got_refs, out_ref = refs
    total = own_ref[...]
    for got_ref in got_refs:
        total = total + got_ref[...]
    pairs, rows = out_ref.shape
    chunk = norm_chunk(rows, pairs)
    query_scale = scale * lax.rsqrt(total[:, rows + chunk : rows + chunk + 1] + epsilon)
    bank_scale = lax.rsqrt(total[:, rows : rows + chunk] + epsilon)
    for row in range(rows // chunk):
        span = slice(row * chunk, (row + 1) * chunk)
        out_ref[:, span] = total[:, span] * query_scale * bank_scale[row : row + 1, :]


def scores(messages, rows, scale):
    pairs = messages[0].shape[0]
    return pl.pallas_call(
        functools.partial(scores_kernel, scale),
        out_shape=jax.ShapeDtypeStruct((pairs, rows), jnp.float32),
        in_specs=[VMEM] * len(messages),
        out_specs=VMEM,
        compiler_params=pltpu.CompilerParams(vmem_limit_bytes=8 << 20),
    )(*messages)


def per_device(hidden, out_grad, proj_in, proj_out, lengths, pair_perm, bank_slab):
    rank = proj_in.shape[0]
    tp_count = lax.axis_size("tp")
    bank_count = lax.axis_size("bank")
    out_away, proj_held, rows_held, live, signs = out_send(
        proj_out, out_grad, lengths, pair_perm, bank_count * tp_count, tp_count
    )
    out_got = lax.ppermute(out_away, "tp", flip(1))
    out_chip = add(out_keep(proj_held, rows_held), out_got, 4)
    out_other = lax.ppermute(out_chip, "tp", flip(2))
    in_away = in_factor(proj_in, hidden, out_chip, 1)
    in_keep = in_factor(proj_in, hidden, in_away, 0)
    in_got = lax.ppermute(in_away, "tp", flip(1))
    out_full = add(out_chip, out_other, 4 * 10**9)
    bank_part = norms(bank_slab, in_away)
    outgoing = outer(
        live, in_keep, in_got, out_full, bank_part, [device % 4 for device in exchange_order(bank_count)]
    )
    partials = lax.all_to_all(
        outgoing, ("bank", "tp"), 0, 0, tiled=True, axis_index_groups=[exchange_order(bank_count)]
    )
    messages = dots(signs, partials, bank_slab, bank_part, tp_count)
    got = [messages[0]] + [lax.ppermute(messages[step], "tp", flip(step)) for step in (2, 3, 1)]
    return scores(got, bank_slab.shape[0], float(rank))


def solution(mesh):
    return jax.shard_map(
        per_device,
        mesh=mesh,
        in_specs=(
            P("bank", None, "tp"),
            P("bank", None, "tp"),
            P(None, "tp"),
            P(None, "tp"),
            P("bank"),
            P(),
            P("bank", "tp"),
        ),
        out_specs=P("tp", "bank"),
        check_vma=False,
    )
```
